256 devices in a mesh: row: 16 (over x, y), col: 16 (over z, core).
Axes of the slice: x: 4, y: 4, z: 8, core: 2. Of those that a mesh axis runs over, the one named last changes fastest.
Arguments:
- tokens: bfloat16 [131072, 128], P('row'), may hold values from -6 to 6
- centroids: bfloat16 [65536, 128], P('col'), may hold values from -6 to 6
- row_mass: float32 [131072], P('row'), may hold values from 0.25 to 4
- col_mass: float32 [65536], P('col'), may hold values from 0.25 to 4
- candidates: int32 [1024, 64], P('row', 'col'), may hold values from 0 to 31, as said below
- counts: int32 [1024, 16], P('row', 'col'), may hold values from 1 to 4, as said below
Outputs:
- query_term_dual_variable: float32 [131072], P('row')
- cluster_dual_variable: float32 [65536], P('col')
- barycenter: bfloat16 [131072, 128], P('row')
The draws below stay inside these ranges and needn't reach their ends.
Inputs may be any that keep to these rules, and one draw needn't show every extreme that they name: `candidates`: for token tile t and column shard c, entries c * 4 to c * 4 + counts[t, c] - 1 of row t are distinct local tile numbers of that shard and the remaining entries of that group are 0. Every centroid tile is listed by some token tile. `counts`: every token tile lists at least one tile of every column shard; the most listed for one token tile and shard is 4, reached in every draw.
All inputs are finite; a program needn't handle non-finite values.
Results may differ from the reference program's by a relative error of at most 0.0081.
Values may be sent and summed in bfloat16 or wider, within the bound.
A program may use at most 64 MiB of HBM per device.

```python
import math
import jax
import jax.numpy as jnp
from jax import lax

VECTOR_DIMENSION = 128
TILE = 128
SLOTS = 4
ITERS = 2
TOK_DEV = 8192
CEN_DEV = 4096
QUERY_TERMS_NUM = 131072
CLUSTER_MEANS_NUM = 65536
N_COL = 16


def shuffle(subkey):
    return jax.random.permutation(subkey, QUERY_TERMS_NUM // TILE)


def candidate_pattern(key):
    tile_total = QUERY_TERMS_NUM // TILE
    local_tiles = CEN_DEV // TILE
    tiles_device = TOK_DEV // TILE
    shard_count = CLUSTER_MEANS_NUM // CEN_DEV
    high_key, count_key, order_key = jax.random.split(key, 3)
    highest = jax.random.randint(high_key, (tile_total // tiles_device, shard_count), 1, SLOTS + 1)
    highest = jnp.repeat(highest, tiles_device, axis=0)
    listed = 1 + jax.random.randint(count_key, (tile_total, shard_count), 0, SLOTS) % highest
    listed = listed.at[0, 0].set(SLOTS)
    order_keys = jax.random.split(order_key, shard_count)
    orders = jax.vmap(shuffle)(order_keys)
    starts = jnp.transpose(orders) % local_tiles
    slot_numbers = jnp.arange(SLOTS, dtype=jnp.int32)
    chosen = (starts[:, :, None] + slot_numbers[None, None, :]) % local_tiles
    chosen = jnp.where(slot_numbers[None, None, :] < listed[:, :, None], chosen, 0)
    return (chosen.reshape(tile_total, shard_count * SLOTS).astype(jnp.int32), listed.astype(jnp.int32))


def draw_candidates(key, part):
    return candidate_pattern(key)[0]


def draw_counts(key, part):
    return candidate_pattern(key)[1]


def shard_offsets(key, strength):
    shard_count = CLUSTER_MEANS_NUM // CEN_DEV
    common_key, own_key, sign_key = jax.random.split(key, 3)
    common = jax.random.normal(common_key, (VECTOR_DIMENSION,), jnp.float32)
    own = jax.random.normal(own_key, (shard_count, VECTOR_DIMENSION), jnp.float32)
    order = jax.random.permutation(sign_key, shard_count)
    signs = jnp.where(order < shard_count // 2, 1.0, -1.0).astype(jnp.float32)
    return strength * (0.8 * signs[:, None] * common[None, :] + 0.6 * own)


def draw_centroids(key, part):
    key = jax.random.fold_in(key, 7)
    shard_count = CLUSTER_MEANS_NUM // CEN_DEV
    base_key, offset_key = jax.random.split(key, 2)
    base = jax.random.normal(base_key, (CLUSTER_MEANS_NUM, VECTOR_DIMENSION), jnp.float32)
    offsets = shard_offsets(offset_key, 0.5)
    shifted = base.reshape(shard_count, CEN_DEV, VECTOR_DIMENSION) + offsets[:, None, :]
    shifted = jnp.clip(shifted, -6.0, 6.0)
    return shifted.reshape(CLUSTER_MEANS_NUM, VECTOR_DIMENSION).astype(jnp.bfloat16)


def steps_of(rng, dims, cuts, low, largest):
    level = 1.0
    for dim, shards_of in cuts:
        draws = jax.random.uniform(jax.random.fold_in(jax.random.fold_in(rng, 6), dim), (shards_of,), jnp.float32, low / len(cuts), largest / len(cuts))
        level = level * jnp.repeat(jnp.exp(draws), dims[dim] // shards_of).reshape((-1,) + (1,) * (len(dims) - 1 - dim))
    return level


def noise(stream_key, extent, width, most, pieces=(), kind=jnp.bfloat16):
    entries = width * jax.random.normal(stream_key, extent, jnp.float32)
    if pieces:
        entries = entries * steps_of(stream_key, extent, pieces, -0.22, 0.18)
    return jnp.clip(entries, -most, most).astype(kind)


def setup_inputs(seed: int = 0) -> dict:
    key_list = jax.random.split(jax.random.key(seed), 7)
    return {
        "tokens": noise(key_list[0], (QUERY_TERMS_NUM, VECTOR_DIMENSION), 1.0, 6.0, ((0, 16),)),
        "centroids": draw_centroids(jax.random.fold_in(key_list[6], 71), 0),
        "row_mass": jnp.clip(jnp.exp(math.log(4.0) - 2.7725887 * jax.random.uniform(key_list[2], (QUERY_TERMS_NUM,), jnp.float32) ** steps_of(key_list[2], (QUERY_TERMS_NUM,), ((0, 16),), -0.2, 0.2)), 0.25, 4.0),
        "col_mass": jnp.clip(jnp.exp(math.log(4.0) - 2.7725887 * jax.random.uniform(key_list[3], (CLUSTER_MEANS_NUM,), jnp.float32) ** steps_of(key_list[3], (CLUSTER_MEANS_NUM,), ((0, 16),), -0.2, 0.2)), 0.25, 4.0),
        "candidates": draw_candidates(jax.random.fold_in(key_list[6], 71), 0),
        "counts": draw_counts(jax.random.fold_in(key_list[6], 71), 0),
    }


entropic_regularizer = 0.025
square_start_position = 0.5

def unit_rows(values):
    widened = values.astype(jnp.float32)
    factor = lax.rsqrt(lax.optimization_barrier(jnp.mean(widened * widened, axis=-1, keepdims=True)) + 1e-06)
    return (widened * factor).astype(jnp.bfloat16)

def reference(tokens, centroids, row_mass, col_mass, candidates, counts):
    token_blocks = unit_rows(tokens).reshape(QUERY_TERMS_NUM // TILE, TILE, VECTOR_DIMENSION)
    centroid_blocks = unit_rows(centroids).reshape(CLUSTER_MEANS_NUM // TILE, TILE, VECTOR_DIMENSION)
    local_tiles = CEN_DEV // TILE
    columns = jnp.arange(N_COL * SLOTS, dtype=jnp.int32)
    owners = columns // SLOTS
    within = columns % SLOTS
    global_ids = (candidates + owners[None, :] * local_tiles).astype(jnp.int32)
    active = within[None, :] < jnp.repeat(counts, SLOTS, axis=1)

    def tile_kernel(inputs):
        block, chosen, alive = inputs
        picked = centroid_blocks[chosen].astype(jnp.float32)
        similarity_values = jnp.einsum('ad,kcd->kac', block.astype(jnp.float32), picked, precision=lax.Precision.HIGHEST)
        gibbs_similarity_matrix = jnp.exp((similarity_values / VECTOR_DIMENSION - square_start_position) / entropic_regularizer)
        return jnp.where(alive[:, None, None], gibbs_similarity_matrix, jnp.zeros_like(gibbs_similarity_matrix))
    kernels = lax.map(tile_kernel, (token_blocks, global_ids, active))
    target_square_numbers = jnp.ones((CLUSTER_MEANS_NUM // TILE, TILE), jnp.float32)
    source_square_numbers = jnp.ones((QUERY_TERMS_NUM // TILE, TILE), jnp.float32)
    for sweep_index in range(ITERS):
        row_sums = jnp.einsum('tkac,tkc->ta', kernels, target_square_numbers[global_ids], precision=lax.Precision.HIGHEST)
        source_square_numbers = row_mass.reshape(-1, TILE) / row_sums
        partial_value = jnp.einsum('tkac,ta->tkc', kernels, source_square_numbers, precision=lax.Precision.HIGHEST)
        col_sums = jax.ops.segment_sum(partial_value.reshape(-1, TILE), global_ids.reshape(-1), num_segments=CLUSTER_MEANS_NUM // TILE)
        target_square_numbers = col_mass.reshape(-1, TILE) / col_sums

    def tile_plan(inputs):
        gibbs_similarity_matrix, chosen, row_scale = inputs
        plan = gibbs_similarity_matrix * row_scale[None, :, None] * target_square_numbers[chosen][:, None, :]
        denominator = lax.optimization_barrier(jnp.sum(plan, axis=(0, 2)))
        rounded = lax.optimization_barrier(plan.astype(jnp.bfloat16)).astype(jnp.float32)
        numerator = jnp.einsum('kac,kcd->ad', rounded, centroid_blocks[chosen].astype(jnp.float32), precision=lax.Precision.HIGHEST)
        return (numerator / denominator[:, None]).astype(jnp.bfloat16)
    barycenter = lax.map(tile_plan, (kernels, global_ids, source_square_numbers)).reshape(QUERY_TERMS_NUM, VECTOR_DIMENSION)
    query_term_dual_variable = entropic_regularizer * jnp.log(source_square_numbers).reshape(QUERY_TERMS_NUM)
    cluster_dual_variable = entropic_regularizer * jnp.log(target_square_numbers).reshape(CLUSTER_MEANS_NUM)
    return (query_term_dual_variable, cluster_dual_variable, barycenter)
```

```python
import functools
import math

import jax
import jax.numpy as jnp
from jax import lax
from jax.experimental import pallas as pl
from jax.experimental.pallas import tpu as pltpu
from jax.sharding import PartitionSpec as P

TILE = 128
SLOTS = 4
ITERS = 2
EPS = 0.025
OFFSET = 0.5
MESH = pl.DeviceIdType.MESH
F32 = jnp.float32
BF16 = jnp.bfloat16
NT = (((1,), (1,)), ((), ()))
TN = (((0,), (0,)), ((), ()))


def unit(values):
    wide = values.astype(F32)
    factor = lax.rsqrt(jnp.mean(wide * wide, axis=-1, keepdims=True) + 1e-06)
    return (wide * factor).astype(BF16)


def spread(row, rows=16):
    return jnp.broadcast_to(row, (rows, TILE)).astype(BF16)


def column(row):
    return jnp.transpose(jnp.broadcast_to(row, (TILE, TILE)))


def remote(src, dst, ss, rs, where):
    copy = pltpu.make_async_remote_copy(
        src_ref=src, dst_ref=dst, send_sem=ss, recv_sem=rs, device_id=where, device_id_type=MESH
    )
    copy.start()
    return copy


def wait_bytes(ref, sem):
    pltpu.make_async_copy(ref, ref, sem).wait()


def kernel(
    nrow, nz, tiles, local, qt,
    cand, cnt, tok, cen, rmass, cmass,
    qd, cd, out,
    cu, kb, cc, hot, psum, pair, zrow, rsc, qsum, crow, csc,
    pd, dpair, dsum, drow, nb, npair, fr, br,
    row_s, col_s, d_s, np_s, np_r, ring_s, ring_r, ag_s, ag_r, sh_s, sh_r,
):
    half = tiles // 2
    hq = qt // 2
    r = lax.axis_index("row")
    k = lax.axis_index("col")
    z = k // 2
    c = k % 2
    o = 1 - c
    partner = {"col": 2 * z + o}
    up = {"col": 2 * lax.rem(z + 1, nz) + c}
    down = {"col": 2 * lax.rem(z + nz - 1, nz) + c}

    barrier = pltpu.get_barrier_semaphore()
    pl.semaphore_signal(barrier, inc=1, device_id=partner, device_id_type=MESH)
    for d in range(1, nz):
        pl.semaphore_signal(
            barrier, inc=1, device_id={"col": 2 * lax.rem(z + d, nz) + c}, device_id_type=MESH
        )
    for d in range(1, nrow):
        pl.semaphore_signal(barrier, inc=1, device_id={"row": lax.rem(r + d, nrow)}, device_id_type=MESH)

    @pl.loop(0, local)
    def _(n):
        at = pl.ds(pl.multiple_of(n * TILE, TILE), TILE)
        cu[n] = unit(cen[at, :])

    lane = lax.broadcasted_iota(jnp.int32, (1, TILE), 1)
    ones = jnp.ones((16, TILE), BF16)
    scale = math.log2(math.e) / (TILE * EPS)
    shift = -OFFSET / EPS * math.log2(math.e)

    for h in range(2):

        @pl.loop(0, half)
        def _(g):
            t = h * half + g
            tu = unit(tok[pl.ds(pl.multiple_of(t * TILE, TILE), TILE), :])
            listed = cnt[t, 0]
            total = None
            for s in range(SLOTS):
                chosen = cand[t, s]
                sim = lax.dot_general(tu, cu[chosen], NT, preferred_element_type=F32)
                base = jnp.minimum(listed - (s + 1), 0).astype(F32) * 1e30 + shift
                gibbs = jnp.exp2(sim * scale + base)
                kb[t, :, s * TILE : (s + 1) * TILE] = gibbs.astype(BF16)
                total = gibbs if total is None else total + gibbs
                hot[s, pl.ds(t, 1), :] = (lane == chosen).astype(F32)
            sums = lax.dot_general(ones, total.astype(BF16), NT, preferred_element_type=F32)
            psum[0, h, pl.ds(g, 1), :] = sums[0:1, :]

    pl.semaphore_wait(barrier, nz + nrow - 1)

    def row_exchange(i):
        remote(psum.at[i, o], pair.at[i], row_s.at[i, 0], row_s.at[i, 1], partner).wait()
        zrow[i, z] = (psum[i, c] + pair[i]).astype(BF16)
        for d in range(1, nz):
            there = {"col": 2 * lax.rem(z + d, nz) + c}
            remote(zrow.at[i, z], zrow.at[i, z], row_s.at[i, 2], row_s.at[i, 3], there)
        wait_bytes(zrow.at[i, pl.ds(0, nz - 1)], row_s.at[i, 3])
        wait_bytes(zrow.at[i, pl.ds(0, nz - 1)], row_s.at[i, 2])
        whole = zrow[i, 0].astype(F32)
        for d in range(1, nz):
            whole = whole + zrow[i, d].astype(F32)
        rsc[i, c] = rmass[c] / whole
        remote(rsc.at[i, c], rsc.at[i, c], row_s.at[i, 4], row_s.at[i, 5], partner).wait()

    def col_exchange(i):
        for d in range(1, nrow):
            remote(crow.at[i, r], crow.at[i, r], col_s.at[i, 0], col_s.at[i, 1], {"row": lax.rem(r + d, nrow)})
        wait_bytes(crow.at[i, pl.ds(0, nrow - 1)], col_s.at[i, 1])
        wait_bytes(crow.at[i, pl.ds(0, nrow - 1)], col_s.at[i, 0])
        whole = crow[i, 0].astype(F32)
        for d in range(1, nrow):
            whole = whole + crow[i, d].astype(F32)
        csc[i] = cmass[...] / whole

    for i in range(ITERS):
        if i > 0:
            scales = jnp.concatenate([csc[i - 1], jnp.zeros((TILE - local, TILE), F32)], axis=0).astype(BF16)
            for s in range(SLOTS):
                qsum[s] = jnp.dot(hot[s].astype(BF16), scales, preferred_element_type=F32)
            for h in range(2):

                @pl.loop(0, half)
                def _(g):
                    t = h * half + g
                    sums = None
                    for s in range(SLOTS):
                        weight = spread(qsum[s, pl.ds(t, 1), :])
                        part = lax.dot_general(
                            weight, kb[t, :, s * TILE : (s + 1) * TILE], NT, preferred_element_type=F32
                        )
                        sums = part if sums is None else sums + part
                    psum[i, h, pl.ds(g, 1), :] = sums[0:1, :]

        row_exchange(i)

        for h in range(2):

            @pl.loop(0, half)
            def _(g):
                t = h * half + g
                weight = spread(rsc[i, h, pl.ds(g, 1), :])
                sums = jnp.dot(weight, kb[t], preferred_element_type=F32)
                for s in range(SLOTS):
                    qsum[s, pl.ds(t, 1), :] = sums[0:1, s * TILE : (s + 1) * TILE]

        whole = jnp.zeros((TILE, TILE), F32)
        for s in range(SLOTS):
            pick = hot[s].astype(BF16)
            high = qsum[s].astype(BF16)
            low = (qsum[s] - high.astype(F32)).astype(BF16)
            whole = whole + lax.dot_general(pick, high, TN, preferred_element_type=F32)
            whole = whole + lax.dot_general(pick, low, TN, preferred_element_type=F32)
        crow[i, r] = whole[0:local, :].astype(BF16)
        col_exchange(i)

    last = ITERS - 1

    @pl.loop(0, local)
    def _(n):
        wide = column(csc[last, pl.ds(n, 1), :] * (1.0 / 16.0))
        cc[n, :, 0:TILE] = (wide * cu[n].astype(F32)).astype(BF16)
        cc[n, :, TILE : 2 * TILE] = wide.astype(BF16)

    diagonal = lax.broadcasted_iota(jnp.int32, (TILE, TILE), 0) == lax.broadcasted_iota(
        jnp.int32, (TILE, TILE), 1
    )

    def numerators(h, g):
        for q in range(qt):
            t = h * half + g * qt + q
            acc = None
            for s in range(SLOTS):
                part = jnp.dot(
                    kb[t, :, s * TILE : (s + 1) * TILE], cc[cand[t, s]], preferred_element_type=F32
                )
                acc = part if acc is None else acc + part
            nb[h, g, q] = acc[:, 0:TILE].astype(BF16)
            mass = jnp.where(diagonal, acc[:, TILE : 2 * TILE], 0.0)
            pd[h, g, q : q + 1, :] = jnp.sum(mass, axis=0, keepdims=True)

    def group(d):
        return lax.rem(z + d, nz)

    sends = []
    far = nz // 2

    order = [far] + [x for j in range(1, far) for x in (far - j, far + j)] + [0]

    def give(j):
        return remote(nb.at[o, group(order[j])], npair.at[group(order[j])], np_s.at[j], np_r.at[j], partner)

    numerators(o, group(far))
    sends.append(give(0))
    numerators(c, group(far))

    def take(j):
        pltpu.make_async_copy(npair.at[0], npair.at[0], np_r.at[j]).wait()

    take(0)
    g = group(far)
    for q in range(qt):
        nb[c, g, q] = (nb[c, g, q].astype(F32) + npair[g, q].astype(F32)).astype(BF16)
    sends.append(remote(nb.at[c, g, pl.ds(0, hq)], fr.at[0, pl.ds(0, hq)], ring_s.at[0, 0, 0], ring_r.at[0, 0, 0], up))
    sends.append(remote(nb.at[c, g, pl.ds(hq, hq)], br.at[0, pl.ds(hq, hq)], ring_s.at[1, 0, 1], ring_r.at[1, 0, 1], down))

    for j in range(1, nz):
        numerators(o, group(order[j]))
        sends.append(give(j))

    @pl.loop(1, nz)
    def _(j):
        numerators(c, lax.rem(z + far + j, nz))

    copy = remote(pd.at[o], dpair, d_s.at[0], d_s.at[1], partner)
    copy.wait()
    dsum[...] = pd[c] + dpair[...]
    drow[z] = dsum[z]
    for d in range(1, nz):
        remote(dsum.at[group(d)], drow.at[z], d_s.at[2], d_s.at[3], {"col": 2 * group(d) + c})

    for step in range(1, far):
        for side, d, buf, to in ((0, far - step, fr, up), (1, far + step, br, down)):
            take(order.index(d))
        for part in range(2):
            for side, d, buf, to in ((0, far - step, fr, up), (1, far + step, br, down)):
                g = group(d)
                came = step > 1 or part == side
                if came:
                    ref = buf.at[step - 1, pl.ds(part * hq, hq)]
                    wait_bytes(ref, ring_r.at[side, step - 1, part])
                for q in range(part * hq, (part + 1) * hq):
                    value = nb[c, g, q].astype(F32) + npair[g, q].astype(F32)
                    if came:
                        value = value + buf[step - 1, q].astype(F32)
                    nb[c, g, q] = value.astype(BF16)
                sends.append(
                    remote(
                        nb.at[c, g, pl.ds(part * hq, hq)], buf.at[step, pl.ds(part * hq, hq)],
                        ring_s.at[side, step, part], ring_r.at[side, step, part], to,
                    )
                )

    wait_bytes(drow.at[pl.ds(0, nz - 1)], d_s.at[3])
    wait_bytes(drow.at[pl.ds(0, nz - 1)], d_s.at[2])
    mass = drow[0]
    for d in range(1, nz):
        mass = mass + drow[d]

    take(order.index(0))
    final = far - 1
    for part in range(2):
        mine = pl.ds(part * hq, hq)
        wait_bytes(fr.at[final, mine], ring_r.at[0, final, part])
        wait_bytes(br.at[final, mine], ring_r.at[1, final, part])
        for q in range(part * hq, (part + 1) * hq):
            value = nb[c, z, q].astype(F32) + npair[z, q].astype(F32)
            value = value + fr[final, q].astype(F32) + br[final, q].astype(F32)
            out[c, z, q] = (value / column(mass[q : q + 1, :])).astype(BF16)
        ref = out.at[c, z, mine]
        sends.append(remote(ref, ref, ag_s.at[0, 0, part], ag_r.at[0, 0, part], up))
        sends.append(remote(ref, ref, ag_s.at[1, 0, part], ag_r.at[1, 0, part], down))
        sends.append(remote(ref, ref, sh_s.at[0, 0, part], sh_r, partner))

    for dist in range(1, far + 1):
        for part in range(2):
            for side, g, to in ((0, group(nz - dist), up), (1, group(dist), down)):
                if dist == far and part != side:
                    continue
                ref = out.at[c, g, pl.ds(part * hq, hq)]
                wait_bytes(ref, ag_r.at[side, dist - 1, part])
                if dist < far - 1 or (dist == far - 1 and part == side):
                    sends.append(remote(ref, ref, ag_s.at[side, dist, part], ag_r.at[side, dist, part], to))
                sends.append(remote(ref, ref, sh_s.at[side, dist, part], sh_r, partner))

    qd[...] = EPS * jnp.log(rsc[last])
    cd[...] = EPS * jnp.log(csc[last])

    wait_bytes(out.at[o], sh_r)
    for copy in sends:
        copy.wait_send()


def shards(nrow, nz, tokens, centroids, row_mass, col_mass, candidates, counts):
    tiles = tokens.shape[0] // TILE
    local = centroids.shape[0] // TILE
    half = tiles // 2
    qt = half // nz
    far = nz // 2
    vmem = pl.BlockSpec(memory_space=pltpu.VMEM)
    smem = pl.BlockSpec(memory_space=pltpu.SMEM)
    dma = pltpu.SemaphoreType.DMA
    qd, cd, out = pl.pallas_call(
        functools.partial(kernel, nrow, nz, tiles, local, qt),
        out_shape=(
            jax.ShapeDtypeStruct((2, half, TILE), F32),
            jax.ShapeDtypeStruct((local, TILE), F32),
            jax.ShapeDtypeStruct((2, nz, qt, TILE, TILE), BF16),
        ),
        in_specs=[smem, smem, vmem, vmem, vmem, vmem],
        out_specs=(vmem, vmem, vmem),
        scratch_shapes=[
            pltpu.VMEM((local, TILE, TILE), BF16),
            pltpu.VMEM((tiles, TILE, SLOTS * TILE), BF16),
            pltpu.VMEM((local, TILE, 2 * TILE), BF16),
            pltpu.VMEM((SLOTS, tiles, TILE), F32),
            pltpu.VMEM((ITERS, 2, half, TILE), F32),
            pltpu.VMEM((ITERS, half, TILE), F32),
            pltpu.VMEM((ITERS, nz, half, TILE), BF16),
            pltpu.VMEM((ITERS, 2, half, TILE), F32),
            pltpu.VMEM((SLOTS, tiles, TILE), F32),
            pltpu.VMEM((ITERS, nrow, local, TILE), BF16),
            pltpu.VMEM((ITERS, local, TILE), F32),
            pltpu.VMEM((2, nz, qt, TILE), F32),
            pltpu.VMEM((nz, qt, TILE), F32),
            pltpu.VMEM((nz, qt, TILE), F32),
            pltpu.VMEM((nz, qt, TILE), F32),
            pltpu.VMEM((2, nz, qt, TILE, TILE), BF16),
            pltpu.VMEM((nz, qt, TILE, TILE), BF16),
            pltpu.VMEM((far, qt, TILE, TILE), BF16),
            pltpu.VMEM((far, qt, TILE, TILE), BF16),
            dma((ITERS, 6)),
            dma((ITERS, 2)),
            dma((4,)),
            dma((nz,)),
            dma((nz,)),
            dma((2, far, 2)),
            dma((2, far, 2)),
            dma((2, far + 1, 2)),
            dma((2, far + 1, 2)),
            dma((2, far + 1, 2)),
            dma(()),
        ],
        compiler_params=pltpu.CompilerParams(
            collective_id=0, has_side_effects=True, vmem_limit_bytes=48 << 20
        ),
    )(
        candidates, counts, tokens, centroids,
        row_mass.reshape(2, half, TILE), col_mass.reshape(local, TILE),
    )
    return qd.reshape(-1), cd.reshape(-1), out.reshape(tokens.shape)


def solution(mesh):
    in_specs = (
        P("row", None),
        P("col", None),
        P("row"),
        P("col"),
        P("row", "col"),
        P("row", "col"),
    )
    out_specs = (P("row"), P("col"), P("row", None))
    body = functools.partial(shards, mesh.shape["row"], mesh.shape["col"] // 2)
    return jax.shard_map(body, mesh=mesh, in_specs=in_specs, out_specs=out_specs, check_vma=False)
```

```python
import functools
import math

import jax
import jax.numpy as jnp
from jax import lax
from jax.experimental import pallas as pl
from jax.experimental.pallas import tpu as pltpu
from jax.sharding import PartitionSpec as P

TILE = 128
SLOTS = 4
ITERS = 2
CHUNKS = 8
EPS = 0.025
OFFSET = 0.5
MESH = pl.DeviceIdType.MESH
F32 = jnp.float32
BF16 = jnp.bfloat16
NT = (((1,), (1,)), ((), ()))
TN = (((0,), (0,)), ((), ()))


def unit(values):
    wide = values.astype(F32)
    factor = lax.rsqrt(jnp.mean(wide * wide, axis=-1, keepdims=True) + 1e-06)
    return (wide * factor).astype(BF16)


def spread(row, rows=16):
    return jnp.broadcast_to(row, (rows, TILE)).astype(BF16)


def column(row):
    return jnp.transpose(jnp.broadcast_to(row, (TILE, TILE)))


def remote(src, dst, ss, rs, where):
    copy = pltpu.make_async_remote_copy(
        src_ref=src, dst_ref=dst, send_sem=ss, recv_sem=rs, device_id=where, device_id_type=MESH
    )
    copy.start()
    return copy


def wait_bytes(ref, sem):
    pltpu.make_async_copy(ref, ref, sem).wait()


def kernel(
    nrow, nz, tiles, local, qt,
    cand, cnt, tok, cen, rmass, cmass,
    qd, cd, out,
    tokv, cenv, cu, kb, cc, hot, psum, pair, zrow, rsc, qsum, crow, csc,
    pd, dpair, dsum, drow, nb, npair, fr, br,
    in_s, row_s, col_s, d_s, d_r, np_s, np_r, ring_s, ring_r, ag_s, ag_r, sh_s, sh_r,
):
    half = tiles // 2
    hq = qt // 2
    r = lax.axis_index("row")
    k = lax.axis_index("col")
    z = k // 2
    c = k % 2
    o = 1 - c
    partner = {"col": 2 * z + o}
    up = {"col": 2 * lax.rem(z + 1, nz) + c}
    down = {"col": 2 * lax.rem(z + nz - 1, nz) + c}

    barrier = pltpu.get_barrier_semaphore()
    pl.semaphore_signal(barrier, inc=1, device_id=partner, device_id_type=MESH)
    for d in range(1, nz):
        pl.semaphore_signal(
            barrier, inc=1, device_id={"col": 2 * lax.rem(z + d, nz) + c}, device_id_type=MESH
        )
    for d in range(1, nrow):
        pl.semaphore_signal(barrier, inc=1, device_id={"row": lax.rem(r + d, nrow)}, device_id_type=MESH)

    chunk = tiles // CHUNKS
    load = pltpu.make_async_copy(cen, cenv, in_s.at[CHUNKS])
    load.start()
    for n in range(CHUNKS):
        at = pl.ds(n * chunk, chunk)
        pltpu.make_async_copy(tok.at[at], tokv.at[at], in_s.at[n]).start()

    load.wait()

    @pl.loop(0, local, unroll=4)
    def _(n):
        cu[n] = unit(cenv[n])

    lane = lax.broadcasted_iota(jnp.int32, (1, TILE), 1)
    scale = math.log2(math.e) / (TILE * EPS)
    shift = -OFFSET / EPS * math.log2(math.e)

    @pl.loop(0, CHUNKS)
    def _(n):
        at = pl.ds(n * chunk, chunk)
        pltpu.make_async_copy(tok.at[at], tokv.at[at], in_s.at[n]).wait()

        @pl.loop(0, chunk, unroll=8)
        def _(m):
            t = n * chunk + m
            tu = unit(tokv[t])
            listed = cnt[0, t]
            chosen = [cand[s, t] for s in range(SLOTS)]
            picked = jnp.concatenate([cu[x] for x in chosen], axis=0)
            sims = lax.dot_general(tu, picked, NT, preferred_element_type=F32)
            total = None
            for s in range(SLOTS):
                base = jnp.minimum(listed - (s + 1), 0).astype(F32) * 1e30 + shift
                gibbs = jnp.exp2(sims[:, s * TILE : (s + 1) * TILE] * scale + base)
                kb[t, :, s * TILE : (s + 1) * TILE] = gibbs.astype(BF16)
                total = gibbs if total is None else total + gibbs
                hot[s, pl.ds(t, 1), :] = (lane == chosen[s]).astype(F32)
            sums = jnp.transpose(jnp.sum(total, axis=1, keepdims=True))
            psum[0, n // (CHUNKS // 2), pl.ds(lax.rem(t, half), 1), :] = sums

    pl.semaphore_wait(barrier, nz + nrow - 1)

    def row_exchange(i):
        remote(psum.at[i, o], pair.at[i], row_s.at[i, 0], row_s.at[i, 1], partner).wait()
        zrow[i, z] = (psum[i, c] + pair[i]).astype(BF16)
        for d in range(1, nz):
            there = {"col": 2 * lax.rem(z + d, nz) + c}
            remote(zrow.at[i, z], zrow.at[i, z], row_s.at[i, 2], row_s.at[i, 3], there)
        wait_bytes(zrow.at[i, pl.ds(0, nz - 1)], row_s.at[i, 3])
        wait_bytes(zrow.at[i, pl.ds(0, nz - 1)], row_s.at[i, 2])
        whole = zrow[i, 0].astype(F32)
        for d in range(1, nz):
            whole = whole + zrow[i, d].astype(F32)
        rsc[i, c] = rmass[c] / whole
        remote(rsc.at[i, c], rsc.at[i, c], row_s.at[i, 4], row_s.at[i, 5], partner).wait()

    def col_exchange(i):
        for d in range(1, nrow):
            remote(crow.at[i, r], crow.at[i, r], col_s.at[i, 0], col_s.at[i, 1], {"row": lax.rem(r + d, nrow)})
        wait_bytes(crow.at[i, pl.ds(0, nrow - 1)], col_s.at[i, 1])
        wait_bytes(crow.at[i, pl.ds(0, nrow - 1)], col_s.at[i, 0])
        whole = crow[i, 0].astype(F32)
        for d in range(1, nrow):
            whole = whole + crow[i, d].astype(F32)
        csc[i] = cmass[...] / whole

    for i in range(ITERS):
        if i > 0:
            scales = jnp.concatenate([csc[i - 1], jnp.zeros((TILE - local, TILE), F32)], axis=0).astype(BF16)
            for s in range(SLOTS):
                qsum[s] = jnp.dot(hot[s].astype(BF16), scales, preferred_element_type=F32)
            for h in range(2):

                @pl.loop(0, half, unroll=8)
                def _(g):
                    t = h * half + g
                    weight = jnp.concatenate([spread(qsum[s, pl.ds(t, 1), :]) for s in range(SLOTS)], axis=1)
                    sums = lax.dot_general(weight, kb[t], NT, preferred_element_type=F32)
                    psum[i, h, pl.ds(g, 1), :] = sums[0:1, :]

        row_exchange(i)

        for h in range(2):

            @pl.loop(0, half, unroll=8)
            def _(g):
                t = h * half + g
                weight = spread(rsc[i, h, pl.ds(g, 1), :])
                sums = jnp.dot(weight, kb[t], preferred_element_type=F32)
                for s in range(SLOTS):
                    qsum[s, pl.ds(t, 1), :] = sums[0:1, s * TILE : (s + 1) * TILE]

        whole = jnp.zeros((TILE, TILE), F32)
        for s in range(SLOTS):
            pick = hot[s].astype(BF16)
            high = qsum[s].astype(BF16)
            low = (qsum[s] - high.astype(F32)).astype(BF16)
            whole = whole + lax.dot_general(pick, high, TN, preferred_element_type=F32)
            whole = whole + lax.dot_general(pick, low, TN, preferred_element_type=F32)
        crow[i, r] = whole[0:local, :].astype(BF16)
        col_exchange(i)

    last = ITERS - 1

    @pl.loop(0, local, unroll=4)
    def _(n):
        wide = column(csc[last, pl.ds(n, 1), :] * (1.0 / 16.0))
        cc[n, :, 0:TILE] = (wide * cu[n].astype(F32)).astype(BF16)
        cc[n, :, TILE : 2 * TILE] = wide.astype(BF16)

    diagonal = lax.broadcasted_iota(jnp.int32, (TILE, TILE), 0) == lax.broadcasted_iota(
        jnp.int32, (TILE, TILE), 1
    )

    def numerators(h, g):
        for q in range(qt):
            t = h * half + g * qt + q
            scaled = jnp.concatenate([cc[cand[s, t]] for s in range(SLOTS)], axis=0)
            acc = jnp.dot(kb[t], scaled, preferred_element_type=F32)
            nb[h, g, q] = acc[:, 0:TILE].astype(BF16)
            mass = jnp.where(diagonal, acc[:, TILE : 2 * TILE], 0.0)
            pd[h, g, q : q + 1, :] = jnp.sum(mass, axis=0, keepdims=True)

    def group(d):
        return lax.rem(z + d, nz)

    sends = []
    far = nz // 2
    order = [far] + [x for j in range(1, far) for x in (far - j, far + j)] + [0]

    def give(d):
        j, g = order.index(d), group(d)
        numerators(o, g)
        sends.append(remote(nb.at[o, g], npair.at[g], np_s.at[j], np_r.at[j], partner))
        sends.append(remote(pd.at[o, g], dpair.at[g], d_s.at[0, j], d_r.at[j], partner))

    def take(d):
        j, g = order.index(d), group(d)
        wait_bytes(npair.at[g], np_r.at[j])
        wait_bytes(dpair.at[g], d_r.at[j])
        dsum[g] = pd[c, g] + dpair[g]
        if d == 0:
            drow[z] = dsum[z]
        else:
            sends.append(remote(dsum.at[g], drow.at[z], d_s.at[1, j], d_r.at[nz], {"col": 2 * g + c}))

    def ring(side, step, q):
        buf, to = ((fr, up), (br, down))[side]
        g = group(far - step if side == 0 else far + step)
        value = nb[c, g, q].astype(F32) + npair[g, q].astype(F32)
        if step > 1 or (step == 1 and (q < hq) == (side == 0)):
            wait_bytes(buf.at[step - 1, q], ring_r.at[side, step - 1, q])
            value = value + buf[step - 1, q].astype(F32)
        nb[c, g, q] = value.astype(BF16)
        sends.append(
            remote(nb.at[c, g, q], buf.at[step, q], ring_s.at[side, step, q], ring_r.at[side, step, q], to)
        )

    first, second = list(range(hq)), list(range(hq, qt))
    give(far)
    numerators(c, group(far))
    give(far - 1)
    take(far)
    for a, b in zip(first, second):
        ring(0, 0, a)
        ring(1, 0, b)
    for step in range(1, far):
        if step > 1:
            give(far - step)
        give(far + step)
        numerators(c, group(far - step))
        numerators(c, group(far + step))
        if step == far - 1:
            give(0)
        take(far - step)
        take(far + step)
        for a, b in zip(second + first, first + second):
            ring(0, step, a)
            ring(1, step, b)
    numerators(c, z)
    take(0)

    wait_bytes(drow.at[pl.ds(0, nz - 1)], d_r.at[nz])
    mass = drow[0]
    for d in range(1, nz):
        mass = mass + drow[d]

    final = far - 1
    for q in range(qt):
        value = nb[c, z, q].astype(F32) + npair[z, q].astype(F32)
        scale_out = 1.0 / column(mass[q : q + 1, :])
        wait_bytes(fr.at[final, q], ring_r.at[0, final, q])
        wait_bytes(br.at[final, q], ring_r.at[1, final, q])
        value = value + fr[final, q].astype(F32) + br[final, q].astype(F32)
        out[c, z, q] = (value * scale_out).astype(BF16)
        ref = out.at[c, z, q]
        sends.append(remote(ref, ref, ag_s.at[0, 0, q], ag_r.at[0, 0, q], up))
        sends.append(remote(ref, ref, ag_s.at[1, 0, q], ag_r.at[1, 0, q], down))
        sends.append(remote(ref, ref, sh_s.at[0, 0, q], sh_r, partner))

    for dist in range(1, far + 1):
        for q in range(qt):
            for side, g, to in ((0, group(nz - dist), up), (1, group(dist), down)):
                longest = (q < hq) == (side == 0)
                if dist == far and not longest:
                    continue
                ref = out.at[c, g, q]
                wait_bytes(ref, ag_r.at[side, dist - 1, q])
                if dist < far - 1 or (dist == far - 1 and longest):
                    sends.append(remote(ref, ref, ag_s.at[side, dist, q], ag_r.at[side, dist, q], to))
                sends.append(remote(ref, ref, sh_s.at[side, dist, q], sh_r, partner))

    qd[...] = EPS * jnp.log(rsc[last])
    cd[...] = EPS * jnp.log(csc[last])

    wait_bytes(out.at[o], sh_r)
    for copy in sends:
        copy.wait_send()


def shards(nrow, nz, tokens, centroids, row_mass, col_mass, candidates, counts):
    tiles = tokens.shape[0] // TILE
    local = centroids.shape[0] // TILE
    half = tiles // 2
    qt = half // nz
    far = nz // 2
    vmem = pl.BlockSpec(memory_space=pltpu.VMEM)
    hbm = pl.BlockSpec(memory_space=pl.ANY)
    smem = pl.BlockSpec(memory_space=pltpu.SMEM)
    dma = pltpu.SemaphoreType.DMA
    qd, cd, out = pl.pallas_call(
        functools.partial(kernel, nrow, nz, tiles, local, qt),
        out_shape=(
            jax.ShapeDtypeStruct((2, half, TILE), F32),
            jax.ShapeDtypeStruct((local, TILE), F32),
            jax.ShapeDtypeStruct((2, nz, qt, TILE, TILE), BF16),
        ),
        in_specs=[smem, smem, hbm, hbm, vmem, vmem],
        out_specs=(vmem, vmem, vmem),
        scratch_shapes=[
            pltpu.VMEM((tiles, TILE, TILE), BF16),
            pltpu.VMEM((local, TILE, TILE), BF16),
            pltpu.VMEM((local, TILE, TILE), BF16),
            pltpu.VMEM((tiles, TILE, SLOTS * TILE), BF16),
            pltpu.VMEM((local, TILE, 2 * TILE), BF16),
            pltpu.VMEM((SLOTS, tiles, TILE), F32),
            pltpu.VMEM((ITERS, 2, half, TILE), F32),
            pltpu.VMEM((ITERS, half, TILE), F32),
            pltpu.VMEM((ITERS, nz, half, TILE), BF16),
            pltpu.VMEM((ITERS, 2, half, TILE), F32),
            pltpu.VMEM((SLOTS, tiles, TILE), F32),
            pltpu.VMEM((ITERS, nrow, local, TILE), BF16),
            pltpu.VMEM((ITERS, local, TILE), F32),
            pltpu.VMEM((2, nz, qt, TILE), F32),
            pltpu.VMEM((nz, qt, TILE), F32),
            pltpu.VMEM((nz, qt, TILE), F32),
            pltpu.VMEM((nz, qt, TILE), F32),
            pltpu.VMEM((2, nz, qt, TILE, TILE), BF16),
            pltpu.VMEM((nz, qt, TILE, TILE), BF16),
            pltpu.VMEM((far, qt, TILE, TILE), BF16),
            pltpu.VMEM((far, qt, TILE, TILE), BF16),
            dma((CHUNKS + 1,)),
            dma((ITERS, 6)),
            dma((ITERS, 2)),
            dma((2, nz)),
            dma((nz + 1,)),
            dma((nz,)),
            dma((nz,)),
            dma((2, far, qt)),
            dma((2, far, qt)),
            dma((2, far + 1, qt)),
            dma((2, far + 1, qt)),
            dma((2, far + 1, qt)),
            dma(()),
        ],
        compiler_params=pltpu.CompilerParams(
            collective_id=0, has_side_effects=True, vmem_limit_bytes=60 << 20
        ),
    )(
        candidates.T, counts.T,
        tokens.reshape(tiles, TILE, TILE), centroids.reshape(local, TILE, TILE),
        row_mass.reshape(2, half, TILE), col_mass.reshape(local, TILE),
    )
    return qd.reshape(-1), cd.reshape(-1), out.reshape(tokens.shape)


def solution(mesh):
    in_specs = (
        P("row", None),
        P("col", None),
        P("row"),
        P("col"),
        P("row", "col"),
        P("row", "col"),
    )
    out_specs = (P("row"), P("col"), P("row", None))
    body = functools.partial(shards, mesh.shape["row"], mesh.shape["col"] // 2)
    return jax.shard_map(body, mesh=mesh, in_specs=in_specs, out_specs=out_specs, check_vma=False)
```

```python
import functools
import math

import jax
import jax.numpy as jnp
from jax import lax
from jax.experimental import pallas as pl
from jax.experimental.pallas import tpu as pltpu
from jax.sharding import PartitionSpec as P

TILE = 128
SLOTS = 4
ITERS = 2
CHUNKS = 8
EPS = 0.025
OFFSET = 0.5
MESH = pl.DeviceIdType.MESH
F32 = jnp.float32
BF16 = jnp.bfloat16
NT = (((1,), (1,)), ((), ()))
TN = (((0,), (0,)), ((), ()))


def unit(values):
    wide = values.astype(F32)
    factor = lax.rsqrt(jnp.mean(wide * wide, axis=-1, keepdims=True) + 1e-06)
    return (wide * factor).astype(BF16)


def spread(row, rows=16):
    return jnp.broadcast_to(row, (rows, TILE)).astype(BF16)


def column(row):
    return jnp.transpose(jnp.broadcast_to(row, (TILE, TILE)))


def remote(src, dst, ss, rs, where):
    copy = pltpu.make_async_remote_copy(
        src_ref=src, dst_ref=dst, send_sem=ss, recv_sem=rs, device_id=where, device_id_type=MESH
    )
    copy.start()
    return copy


def wait_bytes(ref, sem):
    pltpu.make_async_copy(ref, ref, sem).wait()


def kernel(
    nrow, nz, tiles, local, qt,
    cand, cnt, tok, cen, rmass, cmass,
    qd, cd, out,
    tokv, cenv, cu, kb, cc, hot, psum, pair, zrow, rsc, qsum, crow, csc,
    pd, dpair, dsum, drow, nb, npair, fr, br,
    in_s, row_s, col_s, d_s, d_r, np_s, np_r, ring_s, ring_r, ag_s, ag_r, sh_s, sh_r,
):
    half = tiles // 2
    hq = qt // 2
    r = lax.axis_index("row")
    k = lax.axis_index("col")
    z = k // 2
    c = k % 2
    o = 1 - c
    partner = {"col": 2 * z + o}
    up = {"col": 2 * lax.rem(z + 1, nz) + c}
    down = {"col": 2 * lax.rem(z + nz - 1, nz) + c}
    up2 = {"col": 2 * lax.rem(z + 2, nz) + c}
    down2 = {"col": 2 * lax.rem(z + nz - 2, nz) + c}

    barrier = pltpu.get_barrier_semaphore()
    pl.semaphore_signal(barrier, inc=1, device_id=partner, device_id_type=MESH)
    for d in range(1, nz):
        pl.semaphore_signal(
            barrier, inc=1, device_id={"col": 2 * lax.rem(z + d, nz) + c}, device_id_type=MESH
        )
    for d in range(1, nrow):
        pl.semaphore_signal(barrier, inc=1, device_id={"row": lax.rem(r + d, nrow)}, device_id_type=MESH)

    chunk = tiles // CHUNKS
    load = pltpu.make_async_copy(cen, cenv, in_s.at[CHUNKS])
    load.start()
    for n in range(CHUNKS):
        at = pl.ds(n * chunk, chunk)
        pltpu.make_async_copy(tok.at[at], tokv.at[at], in_s.at[n]).start()

    load.wait()

    @pl.loop(0, local, unroll=4)
    def _(n):
        cu[n] = unit(cenv[n])

    lane = lax.broadcasted_iota(jnp.int32, (1, TILE), 1)
    scale = math.log2(math.e) / (TILE * EPS)
    shift = -OFFSET / EPS * math.log2(math.e)

    @pl.loop(0, CHUNKS)
    def _(n):
        at = pl.ds(n * chunk, chunk)
        pltpu.make_async_copy(tok.at[at], tokv.at[at], in_s.at[n]).wait()

        @pl.loop(0, chunk, unroll=8)
        def _(m):
            t = n * chunk + m
            tu = unit(tokv[t])
            listed = cnt[0, t]
            chosen = [cand[s, t] for s in range(SLOTS)]
            picked = jnp.concatenate([cu[x] for x in chosen], axis=0)
            sims = lax.dot_general(tu, picked, NT, preferred_element_type=F32)
            total = None
            for s in range(SLOTS):
                base = jnp.minimum(listed - (s + 1), 0).astype(F32) * 1e30 + shift
                gibbs = jnp.exp2(sims[:, s * TILE : (s + 1) * TILE] * scale + base)
                kb[t, :, s * TILE : (s + 1) * TILE] = gibbs.astype(BF16)
                total = gibbs if total is None else total + gibbs
                hot[s, pl.ds(t, 1), :] = (lane == chosen[s]).astype(F32)
            sums = jnp.transpose(jnp.sum(total, axis=1, keepdims=True))
            psum[0, n // (CHUNKS // 2), pl.ds(lax.rem(t, half), 1), :] = sums

    pl.semaphore_wait(barrier, nz + nrow - 1)

    def row_exchange(i):
        remote(psum.at[i, o], pair.at[i], row_s.at[i, 0], row_s.at[i, 1], partner).wait()
        zrow[i, z] = (psum[i, c] + pair[i]).astype(BF16)
        for d in range(1, nz):
            there = {"col": 2 * lax.rem(z + d, nz) + c}
            remote(zrow.at[i, z], zrow.at[i, z], row_s.at[i, 2], row_s.at[i, 3], there)
        wait_bytes(zrow.at[i, pl.ds(0, nz - 1)], row_s.at[i, 3])
        wait_bytes(zrow.at[i, pl.ds(0, nz - 1)], row_s.at[i, 2])
        whole = zrow[i, 0].astype(F32)
        for d in range(1, nz):
            whole = whole + zrow[i, d].astype(F32)
        rsc[i, c] = rmass[c] / whole
        remote(rsc.at[i, c], rsc.at[i, c], row_s.at[i, 4], row_s.at[i, 5], partner).wait()

    def col_exchange(i):
        for d in range(1, nrow):
            remote(crow.at[i, r], crow.at[i, r], col_s.at[i, 0], col_s.at[i, 1], {"row": lax.rem(r + d, nrow)})
        wait_bytes(crow.at[i, pl.ds(0, nrow - 1)], col_s.at[i, 1])
        wait_bytes(crow.at[i, pl.ds(0, nrow - 1)], col_s.at[i, 0])
        whole = crow[i, 0].astype(F32)
        for d in range(1, nrow):
            whole = whole + crow[i, d].astype(F32)
        csc[i] = cmass[...] / whole

    for i in range(ITERS):
        if i > 0:
            scales = jnp.concatenate([csc[i - 1], jnp.zeros((TILE - local, TILE), F32)], axis=0).astype(BF16)
            for s in range(SLOTS):
                qsum[s] = jnp.dot(hot[s].astype(BF16), scales, preferred_element_type=F32)
            for h in range(2):

                @pl.loop(0, half, unroll=8)
                def _(g):
                    t = h * half + g
                    weight = jnp.concatenate([spread(qsum[s, pl.ds(t, 1), :]) for s in range(SLOTS)], axis=1)
                    sums = lax.dot_general(weight, kb[t], NT, preferred_element_type=F32)
                    psum[i, h, pl.ds(g, 1), :] = sums[0:1, :]

        row_exchange(i)

        for h in range(2):

            @pl.loop(0, half, unroll=8)
            def _(g):
                t = h * half + g
                weight = spread(rsc[i, h, pl.ds(g, 1), :])
                sums = jnp.dot(weight, kb[t], preferred_element_type=F32)
                for s in range(SLOTS):
                    qsum[s, pl.ds(t, 1), :] = sums[0:1, s * TILE : (s + 1) * TILE]

        whole = jnp.zeros((TILE, TILE), F32)
        for s in range(SLOTS):
            pick = hot[s].astype(BF16)
            high = qsum[s].astype(BF16)
            low = (qsum[s] - high.astype(F32)).astype(BF16)
            whole = whole + lax.dot_general(pick, high, TN, preferred_element_type=F32)
            whole = whole + lax.dot_general(pick, low, TN, preferred_element_type=F32)
        crow[i, r] = whole[0:local, :].astype(BF16)
        col_exchange(i)

    last = ITERS - 1

    @pl.loop(0, local, unroll=4)
    def _(n):
        wide = column(csc[last, pl.ds(n, 1), :] * (1.0 / 16.0))
        cc[n, :, 0:TILE] = (wide * cu[n].astype(F32)).astype(BF16)
        cc[n, :, TILE : 2 * TILE] = wide.astype(BF16)

    diagonal = lax.broadcasted_iota(jnp.int32, (TILE, TILE), 0) == lax.broadcasted_iota(
        jnp.int32, (TILE, TILE), 1
    )

    def numerators(h, g):
        for q in range(qt):
            t = h * half + g * qt + q
            scaled = jnp.concatenate([cc[cand[s, t]] for s in range(SLOTS)], axis=0)
            acc = jnp.dot(kb[t], scaled, preferred_element_type=F32)
            nb[h, g, q] = acc[:, 0:TILE].astype(BF16)
            mass = jnp.where(diagonal, acc[:, TILE : 2 * TILE], 0.0)
            pd[h, g, q : q + 1, :] = jnp.sum(mass, axis=0, keepdims=True)

    def group(d):
        return lax.rem(z + d, nz)

    sends = []
    far = nz // 2
    order = [far] + [x for j in range(1, far) for x in (far - j, far + j)] + [0]

    def give(d):
        j, g = order.index(d), group(d)
        numerators(o, g)
        sends.append(remote(nb.at[o, g], npair.at[g], np_s.at[j], np_r.at[j], partner))
        sends.append(remote(pd.at[o, g], dpair.at[g], d_s.at[0, j], d_r.at[j], partner))

    def take(d):
        j, g = order.index(d), group(d)
        wait_bytes(npair.at[g], np_r.at[j])
        wait_bytes(dpair.at[g], d_r.at[j])
        dsum[g] = pd[c, g] + dpair[g]
        if d == 0:
            drow[z] = dsum[z]
        else:
            sends.append(remote(dsum.at[g], drow.at[z], d_s.at[1, j], d_r.at[nz], {"col": 2 * g + c}))

    def ring(side, step, q):
        buf = (fr, br)[side]
        to = ((up2, down2) if step == 0 else (up, down))[side]
        g = group(far - step if side == 0 else far + step)
        value = nb[c, g, q].astype(F32) + npair[g, q].astype(F32)
        came = [step - 1] if step > 1 else []
        if step == 2 and (q < hq) == (side == 0):
            came.append(0)
        for n in came:
            wait_bytes(buf.at[n, q], ring_r.at[side, n, q])
            value = value + buf[n, q].astype(F32)
        nb[c, g, q] = value.astype(BF16)
        sends.append(
            remote(nb.at[c, g, q], buf.at[step, q], ring_s.at[side, step, q], ring_r.at[side, step, q], to)
        )

    first, second = list(range(hq)), list(range(hq, qt))
    give(far)
    numerators(c, group(far))
    give(far - 1)
    take(far)
    for a, b in zip(first, second):
        ring(0, 0, a)
        ring(1, 0, b)
    for step in range(1, far):
        if step > 1:
            give(far - step)
        give(far + step)
        numerators(c, group(far - step))
        numerators(c, group(far + step))
        if step == far - 1:
            give(0)
        take(far - step)
        take(far + step)
        for a, b in zip(second + first, first + second):
            ring(0, step, a)
            ring(1, step, b)
    numerators(c, z)
    take(0)

    wait_bytes(drow.at[pl.ds(0, nz - 1)], d_r.at[nz])
    mass = drow[0]
    for d in range(1, nz):
        mass = mass + drow[d]

    final = far - 1
    for q in range(qt):
        value = nb[c, z, q].astype(F32) + npair[z, q].astype(F32)
        scale_out = 1.0 / column(mass[q : q + 1, :])
        wait_bytes(fr.at[final, q], ring_r.at[0, final, q])
        wait_bytes(br.at[final, q], ring_r.at[1, final, q])
        value = value + fr[final, q].astype(F32) + br[final, q].astype(F32)
        out[c, z, q] = (value * scale_out).astype(BF16)
        ref = out.at[c, z, q]
        sends.append(remote(ref, ref, ag_s.at[0, 0, q], ag_r.at[0, 0, q], up))
        sends.append(remote(ref, ref, ag_s.at[1, 0, q], ag_r.at[1, 0, q], down))

    def share(n, ref):
        sends.append(remote(ref, ref, sh_s.at[n], sh_r, partner))

    share(0, out.at[c, z])
    for dist in range(1, far + 1):
        for q in range(qt):
            for side, g, to, to2 in ((0, group(nz - dist), up, up2), (1, group(dist), down, down2)):
                longest = (q < hq) == (side == 0)
                if dist == far and not longest:
                    continue
                ref = out.at[c, g, q]
                wait_bytes(ref, ag_r.at[side, dist - 1, q])
                if dist == far - 2 and longest:
                    sends.append(remote(ref, ref, ag_s.at[side, far - 1, q], ag_r.at[side, far - 1, q], to2))
                if dist < far - 1:
                    sends.append(remote(ref, ref, ag_s.at[side, dist, q], ag_r.at[side, dist, q], to))
        if dist < far:
            share(2 * dist - 1, out.at[c, group(nz - dist)])
            share(2 * dist, out.at[c, group(dist)])
        else:
            share(2 * far - 1, out.at[c, group(far)])

    qd[...] = EPS * jnp.log(rsc[last])
    cd[...] = EPS * jnp.log(csc[last])

    wait_bytes(out.at[o], sh_r)
    for copy in sends:
        copy.wait_send()


def shards(nrow, nz, tokens, centroids, row_mass, col_mass, candidates, counts):
    tiles = tokens.shape[0] // TILE
    local = centroids.shape[0] // TILE
    half = tiles // 2
    qt = half // nz
    far = nz // 2
    vmem = pl.BlockSpec(memory_space=pltpu.VMEM)
    hbm = pl.BlockSpec(memory_space=pltpu.HBM)
    smem = pl.BlockSpec(memory_space=pltpu.SMEM)
    dma = pltpu.SemaphoreType.DMA
    qd, cd, out = pl.pallas_call(
        functools.partial(kernel, nrow, nz, tiles, local, qt),
        out_shape=(
            jax.ShapeDtypeStruct((2, half, TILE), F32),
            jax.ShapeDtypeStruct((local, TILE), F32),
            jax.ShapeDtypeStruct((2, nz, qt, TILE, TILE), BF16),
        ),
        in_specs=[smem, smem, hbm, hbm, vmem, vmem],
        out_specs=(vmem, vmem, vmem),
        scratch_shapes=[
            pltpu.VMEM((tiles, TILE, TILE), BF16),
            pltpu.VMEM((local, TILE, TILE), BF16),
            pltpu.VMEM((local, TILE, TILE), BF16),
            pltpu.VMEM((tiles, TILE, SLOTS * TILE), BF16),
            pltpu.VMEM((local, TILE, 2 * TILE), BF16),
            pltpu.VMEM((SLOTS, tiles, TILE), F32),
            pltpu.VMEM((ITERS, 2, half, TILE), F32),
            pltpu.VMEM((ITERS, half, TILE), F32),
            pltpu.VMEM((ITERS, nz, half, TILE), BF16),
            pltpu.VMEM((ITERS, 2, half, TILE), F32),
            pltpu.VMEM((SLOTS, tiles, TILE), F32),
            pltpu.VMEM((ITERS, nrow, local, TILE), BF16),
            pltpu.VMEM((ITERS, local, TILE), F32),
            pltpu.VMEM((2, nz, qt, TILE), F32),
            pltpu.VMEM((nz, qt, TILE), F32),
            pltpu.VMEM((nz, qt, TILE), F32),
            pltpu.VMEM((nz, qt, TILE), F32),
            pltpu.VMEM((2, nz, qt, TILE, TILE), BF16),
            pltpu.VMEM((nz, qt, TILE, TILE), BF16),
            pltpu.VMEM((far, qt, TILE, TILE), BF16),
            pltpu.VMEM((far, qt, TILE, TILE), BF16),
            dma((CHUNKS + 1,)),
            dma((ITERS, 6)),
            dma((ITERS, 2)),
            dma((2, nz)),
            dma((nz + 1,)),
            dma((nz,)),
            dma((nz,)),
            dma((2, far, qt)),
            dma((2, far, qt)),
            dma((2, far, qt)),
            dma((2, far, qt)),
            dma((nz,)),
            dma(()),
        ],
        compiler_params=pltpu.CompilerParams(
            collective_id=0, has_side_effects=True, vmem_limit_bytes=36 << 20
        ),
    )(
        *(
            pltpu.with_memory_space_constraint(x, pltpu.HBM)
            for x in (
                candidates.T, counts.T,
                tokens.reshape(tiles, TILE, TILE), centroids.reshape(local, TILE, TILE),
                row_mass.reshape(2, half, TILE), col_mass.reshape(local, TILE),
            )
        )
    )
    return qd.reshape(-1), cd.reshape(-1), out.reshape(tokens.shape)


def solution(mesh):
    in_specs = (
        P("row", None),
        P("col", None),
        P("row"),
        P("col"),
        P("row", "col"),
        P("row", "col"),
    )
    out_specs = (P("row"), P("col"), P("row", None))
    body = functools.partial(shards, mesh.shape["row"], mesh.shape["col"] // 2)
    return jax.shard_map(body, mesh=mesh, in_specs=in_specs, out_specs=out_specs, check_vma=False)
```

```python
import functools
import math

import jax
import jax.numpy as jnp
from jax import lax
from jax.experimental import pallas as pl
from jax.experimental.pallas import tpu as pltpu
from jax.sharding import PartitionSpec as P

TILE = 128
SLOTS = 4
ITERS = 2
CHUNKS = 8
EPS = 0.025
OFFSET = 0.5
MESH = pl.DeviceIdType.MESH
F32 = jnp.float32
BF16 = jnp.bfloat16
NT = (((1,), (1,)), ((), ()))
TN = (((0,), (0,)), ((), ()))


def unit(values):
    wide = values.astype(F32)
    factor = lax.rsqrt(jnp.mean(wide * wide, axis=-1, keepdims=True) + 1e-06)
    return (wide * factor).astype(BF16)


def spread(row, rows=16):
    return jnp.broadcast_to(row, (rows, TILE)).astype(BF16)


def column(row):
    return jnp.transpose(jnp.broadcast_to(row, (TILE, TILE)))


def remote(src, dst, ss, rs, where):
    copy = pltpu.make_async_remote_copy(
        src_ref=src, dst_ref=dst, send_sem=ss, recv_sem=rs, device_id=where, device_id_type=MESH
    )
    copy.start()
    return copy


def wait_bytes(ref, sem):
    pltpu.make_async_copy(ref, ref, sem).wait()


def kernel(
    nrow, nz, tiles, local, qt,
    cand, cnt, tok, cen, rmass, cmass,
    qd, cd, out,
    tokv, cenv, rmv, cmv, cu, kb, cc, hot, psum, pair, zrow, rsc, qsum, crow, csc,
    pd, dpair, dsum, drow, nb, npair, fr, br,
    in_s, row_s, col_s, d_s, d_r, np_s, np_r, ring_s, ring_r, ag_s, ag_r, sh_s, sh_r,
):
    half = tiles // 2
    hq = qt // 2
    r = lax.axis_index("row")
    k = lax.axis_index("col")
    z = k // 2
    c = k % 2
    o = 1 - c
    partner = {"col": 2 * z + o}
    up = {"col": 2 * lax.rem(z + 1, nz) + c}
    down = {"col": 2 * lax.rem(z + nz - 1, nz) + c}
    up2 = {"col": 2 * lax.rem(z + 2, nz) + c}
    down2 = {"col": 2 * lax.rem(z + nz - 2, nz) + c}

    barrier = pltpu.get_barrier_semaphore()
    pl.semaphore_signal(barrier, inc=1, device_id=partner, device_id_type=MESH)
    for d in range(1, nz):
        pl.semaphore_signal(
            barrier, inc=1, device_id={"col": 2 * lax.rem(z + d, nz) + c}, device_id_type=MESH
        )
    for d in range(1, nrow):
        pl.semaphore_signal(barrier, inc=1, device_id={"row": lax.rem(r + d, nrow)}, device_id_type=MESH)

    chunk = tiles // CHUNKS
    load = pltpu.make_async_copy(cen, cenv, in_s.at[CHUNKS])
    load.start()
    for h in (o, c):
        for n in range(CHUNKS // 2):
            at = pl.ds(h * half + n * chunk, chunk)
            pltpu.make_async_copy(tok.at[at], tokv.at[at], in_s.at[h * (CHUNKS // 2) + n]).start()
    masses = [
        pltpu.make_async_copy(rmass, rmv, in_s.at[CHUNKS + 1]),
        pltpu.make_async_copy(cmass, cmv, in_s.at[CHUNKS + 2]),
    ]
    for copy in masses:
        copy.start()

    load.wait()

    @pl.loop(0, local, unroll=4)
    def _(n):
        cu[n] = unit(cenv[n])

    lane = lax.broadcasted_iota(jnp.int32, (1, TILE), 1)
    scale = math.log2(math.e) / (TILE * EPS)
    shift = -OFFSET / EPS * math.log2(math.e)

    def fill(h):
        @pl.loop(0, CHUNKS // 2)
        def _(n):
            first = h * half + n * chunk
            at = pl.ds(first, chunk)
            pltpu.make_async_copy(tok.at[at], tokv.at[at], in_s.at[h * (CHUNKS // 2) + n]).wait()

            @pl.loop(0, chunk, unroll=8)
            def _(m):
                one_tile(h, n * chunk + m, first + m)

    def one_tile(h, g, t):
        tu = unit(tokv[t])
        listed = cnt[0, t]
        chosen = [cand[s, t] for s in range(SLOTS)]
        picked = jnp.concatenate([cu[x] for x in chosen], axis=0)
        sims = lax.dot_general(tu, picked, NT, preferred_element_type=F32)
        total = None
        for s in range(SLOTS):
            base = jnp.minimum(listed - (s + 1), 0).astype(F32) * 1e30 + shift
            gibbs = jnp.exp2(sims[:, s * TILE : (s + 1) * TILE] * scale + base)
            kb[t, :, s * TILE : (s + 1) * TILE] = gibbs.astype(BF16)
            total = gibbs if total is None else total + gibbs
            hot[s, pl.ds(t, 1), :] = (lane == chosen[s]).astype(F32)
        sums = jnp.transpose(jnp.sum(total, axis=1, keepdims=True))
        psum[0, h, pl.ds(g, 1), :] = sums

    def row_send(i):
        return remote(psum.at[i, o], pair.at[i], row_s.at[i, 0], row_s.at[i, 1], partner)

    def row_exchange(i, sent):
        sent.wait()
        zrow[i, z] = (psum[i, c] + pair[i]).astype(BF16)
        for d in range(1, nz):
            there = {"col": 2 * lax.rem(z + d, nz) + c}
            remote(zrow.at[i, z], zrow.at[i, z], row_s.at[i, 2], row_s.at[i, 3], there)
        wait_bytes(zrow.at[i, pl.ds(0, nz - 1)], row_s.at[i, 3])
        whole = zrow[i, 0].astype(F32)
        for d in range(1, nz):
            whole = whole + zrow[i, d].astype(F32)
        rsc[i, c] = rmv[c] / whole
        shared = remote(rsc.at[i, c], rsc.at[i, c], row_s.at[i, 4], row_s.at[i, 5], partner)
        wait_bytes(zrow.at[i, pl.ds(0, nz - 1)], row_s.at[i, 2])
        return shared

    fill(o)
    pl.semaphore_wait(barrier, nz + nrow - 1)
    sent = row_send(0)
    fill(c)
    for copy in masses:
        copy.wait()

    def col_exchange(i):
        for d in range(1, nrow):
            remote(crow.at[i, r], crow.at[i, r], col_s.at[i, 0], col_s.at[i, 1], {"row": lax.rem(r + d, nrow)})
        wait_bytes(crow.at[i, pl.ds(0, nrow - 1)], col_s.at[i, 1])
        wait_bytes(crow.at[i, pl.ds(0, nrow - 1)], col_s.at[i, 0])
        whole = crow[i, 0].astype(F32)
        for d in range(1, nrow):
            whole = whole + crow[i, d].astype(F32)
        csc[i] = cmv[...] / whole

    for i in range(ITERS):
        if i > 0:
            scales = jnp.concatenate([csc[i - 1], jnp.zeros((TILE - local, TILE), F32)], axis=0).astype(BF16)
            for s in range(SLOTS):
                qsum[s] = jnp.dot(hot[s].astype(BF16), scales, preferred_element_type=F32)

            def row_pass(h):
                @pl.loop(0, half, unroll=8)
                def _(g):
                    t = h * half + g
                    weight = jnp.concatenate([spread(qsum[s, pl.ds(t, 1), :]) for s in range(SLOTS)], axis=1)
                    sums = lax.dot_general(weight, kb[t], NT, preferred_element_type=F32)
                    psum[i, h, pl.ds(g, 1), :] = sums[0:1, :]

            row_pass(o)
            sent = row_send(i)
            row_pass(c)

        shared = row_exchange(i, sent)

        def col_pass(h):
            @pl.loop(0, half, unroll=8)
            def _(g):
                t = h * half + g
                weight = spread(rsc[i, h, pl.ds(g, 1), :])
                sums = jnp.dot(weight, kb[t], preferred_element_type=F32)
                for s in range(SLOTS):
                    qsum[s, pl.ds(t, 1), :] = sums[0:1, s * TILE : (s + 1) * TILE]

        col_pass(c)
        shared.wait()
        col_pass(o)
        whole = jnp.zeros((TILE, TILE), F32)
        for s in range(SLOTS):
            pick = hot[s].astype(BF16)
            high = qsum[s].astype(BF16)
            low = (qsum[s] - high.astype(F32)).astype(BF16)
            whole = whole + lax.dot_general(pick, high, TN, preferred_element_type=F32)
            whole = whole + lax.dot_general(pick, low, TN, preferred_element_type=F32)
        crow[i, r] = whole[0:local, :].astype(BF16)
        col_exchange(i)

    last = ITERS - 1

    @pl.loop(0, local, unroll=4)
    def _(n):
        wide = column(csc[last, pl.ds(n, 1), :] * (1.0 / 16.0))
        cc[n, :, 0:TILE] = (wide * cu[n].astype(F32)).astype(BF16)
        cc[n, :, TILE : 2 * TILE] = wide.astype(BF16)

    diagonal = lax.broadcasted_iota(jnp.int32, (TILE, TILE), 0) == lax.broadcasted_iota(
        jnp.int32, (TILE, TILE), 1
    )

    def numerators(h, g):
        for q in range(qt):
            t = h * half + g * qt + q
            scaled = jnp.concatenate([cc[cand[s, t]] for s in range(SLOTS)], axis=0)
            acc = jnp.dot(kb[t], scaled, preferred_element_type=F32)
            nb[h, g, q] = acc[:, 0:TILE].astype(BF16)
            mass = jnp.where(diagonal, acc[:, TILE : 2 * TILE], 0.0)
            pd[h, g, q : q + 1, :] = jnp.sum(mass, axis=0, keepdims=True)

    def group(d):
        return lax.rem(z + d, nz)

    sends = []
    far = nz // 2
    order = [far] + [x for j in range(1, far) for x in (far - j, far + j)] + [0]

    def give(d):
        j, g = order.index(d), group(d)
        numerators(o, g)
        sends.append(remote(nb.at[o, g], npair.at[g], np_s.at[j], np_r.at[j], partner))
        sends.append(remote(pd.at[o, g], dpair.at[g], d_s.at[0, j], d_r.at[j], partner))

    def take(d):
        j, g = order.index(d), group(d)
        wait_bytes(npair.at[g], np_r.at[j])
        wait_bytes(dpair.at[g], d_r.at[j])
        dsum[g] = pd[c, g] + dpair[g]
        if d == 0:
            drow[z] = dsum[z]
        else:
            sends.append(remote(dsum.at[g], drow.at[z], d_s.at[1, j], d_r.at[nz], {"col": 2 * g + c}))

    def ring(side, step, q):
        buf = (fr, br)[side]
        to = ((up2, down2) if step == 0 else (up, down))[side]
        g = group(far - step if side == 0 else far + step)
        value = nb[c, g, q].astype(F32) + npair[g, q].astype(F32)
        came = [step - 1] if step > 1 else []
        if step == 2 and (q < hq) == (side == 0):
            came.append(0)
        for n in came:
            wait_bytes(buf.at[n, q], ring_r.at[side, n, q])
            value = value + buf[n, q].astype(F32)
        nb[c, g, q] = value.astype(BF16)
        sends.append(
            remote(nb.at[c, g, q], buf.at[step, q], ring_s.at[side, step, q], ring_r.at[side, step, q], to)
        )

    first, second = list(range(hq)), list(range(hq, qt))
    give(far)
    give(far - 1)
    give(far + 1)
    numerators(c, group(far))
    take(far)
    for a, b in zip(first, second):
        ring(0, 0, a)
        ring(1, 0, b)
    for step in range(1, far):
        if step > 1:
            give(far - step)
            give(far + step)
        numerators(c, group(far - step))
        numerators(c, group(far + step))
        if step == far - 1:
            give(0)
        take(far - step)
        take(far + step)
        for a, b in zip(second + first, first + second):
            ring(0, step, a)
            ring(1, step, b)
    numerators(c, z)
    take(0)

    wait_bytes(drow.at[pl.ds(0, nz - 1)], d_r.at[nz])
    mass = drow[0]
    for d in range(1, nz):
        mass = mass + drow[d]

    final = far - 1
    for q in range(qt):
        value = nb[c, z, q].astype(F32) + npair[z, q].astype(F32)
        scale_out = 1.0 / column(mass[q : q + 1, :])
        wait_bytes(fr.at[final, q], ring_r.at[0, final, q])
        wait_bytes(br.at[final, q], ring_r.at[1, final, q])
        value = value + fr[final, q].astype(F32) + br[final, q].astype(F32)
        out[c, z, q] = (value * scale_out).astype(BF16)
        ref = out.at[c, z, q]
        sends.append(remote(ref, ref, ag_s.at[0, 0, q], ag_r.at[0, 0, q], up))
        sends.append(remote(ref, ref, ag_s.at[1, 0, q], ag_r.at[1, 0, q], down))

    def share(n, ref):
        sends.append(remote(ref, ref, sh_s.at[n], sh_r, partner))

    share(0, out.at[c, z])
    for dist in range(1, far + 1):
        for q in range(qt):
            for side, g, to, to2 in ((0, group(nz - dist), up, up2), (1, group(dist), down, down2)):
                longest = (q < hq) == (side == 0)
                if dist == far and not longest:
                    continue
                ref = out.at[c, g, q]
                wait_bytes(ref, ag_r.at[side, dist - 1, q])
                if dist == far - 2 and longest:
                    sends.append(remote(ref, ref, ag_s.at[side, far - 1, q], ag_r.at[side, far - 1, q], to2))
                if dist < far - 1:
                    sends.append(remote(ref, ref, ag_s.at[side, dist, q], ag_r.at[side, dist, q], to))
        if dist < far:
            share(2 * dist - 1, out.at[c, group(nz - dist)])
            share(2 * dist, out.at[c, group(dist)])
        else:
            share(2 * far - 1, out.at[c, group(far)])

    qd[...] = EPS * jnp.log(rsc[last])
    cd[...] = EPS * jnp.log(csc[last])

    wait_bytes(out.at[o], sh_r)
    for copy in sends:
        copy.wait_send()


def shards(nrow, nz, tokens, centroids, row_mass, col_mass, candidates, counts):
    tiles = tokens.shape[0] // TILE
    local = centroids.shape[0] // TILE
    half = tiles // 2
    qt = half // nz
    far = nz // 2
    vmem = pl.BlockSpec(memory_space=pltpu.VMEM)
    hbm = pl.BlockSpec(memory_space=pltpu.HBM)
    smem = pl.BlockSpec(memory_space=pltpu.SMEM)
    dma = pltpu.SemaphoreType.DMA
    qd, cd, out = pl.pallas_call(
        functools.partial(kernel, nrow, nz, tiles, local, qt),
        out_shape=(
            jax.ShapeDtypeStruct((2, half, TILE), F32),
            jax.ShapeDtypeStruct((local, TILE), F32),
            jax.ShapeDtypeStruct((2, nz, qt, TILE, TILE), BF16),
        ),
        in_specs=[smem, smem, hbm, hbm, hbm, hbm],
        out_specs=(vmem, vmem, vmem),
        scratch_shapes=[
            pltpu.VMEM((tiles, TILE, TILE), BF16),
            pltpu.VMEM((local, TILE, TILE), BF16),
            pltpu.VMEM((2, half, TILE), F32),
            pltpu.VMEM((local, TILE), F32),
            pltpu.VMEM((local, TILE, TILE), BF16),
            pltpu.VMEM((tiles, TILE, SLOTS * TILE), BF16),
            pltpu.VMEM((local, TILE, 2 * TILE), BF16),
            pltpu.VMEM((SLOTS, tiles, TILE), F32),
            pltpu.VMEM((ITERS, 2, half, TILE), F32),
            pltpu.VMEM((ITERS, half, TILE), F32),
            pltpu.VMEM((ITERS, nz, half, TILE), BF16),
            pltpu.VMEM((ITERS, 2, half, TILE), F32),
            pltpu.VMEM((SLOTS, tiles, TILE), F32),
            pltpu.VMEM((ITERS, nrow, local, TILE), BF16),
            pltpu.VMEM((ITERS, local, TILE), F32),
            pltpu.VMEM((2, nz, qt, TILE), F32),
            pltpu.VMEM((nz, qt, TILE), F32),
            pltpu.VMEM((nz, qt, TILE), F32),
            pltpu.VMEM((nz, qt, TILE), F32),
            pltpu.VMEM((2, nz, qt, TILE, TILE), BF16),
            pltpu.VMEM((nz, qt, TILE, TILE), BF16),
            pltpu.VMEM((far, qt, TILE, TILE), BF16),
            pltpu.VMEM((far, qt, TILE, TILE), BF16),
            dma((CHUNKS + 3,)),
            dma((ITERS, 6)),
            dma((ITERS, 2)),
            dma((2, nz)),
            dma((nz + 1,)),
            dma((nz,)),
            dma((nz,)),
            dma((2, far, qt)),
            dma((2, far, qt)),
            dma((2, far, qt)),
            dma((2, far, qt)),
            dma((nz,)),
            dma(()),
        ],
        compiler_params=pltpu.CompilerParams(
            collective_id=0, has_side_effects=True, vmem_limit_bytes=36 << 20
        ),
    )(
        *(
            pltpu.with_memory_space_constraint(x, pltpu.HBM)
            for x in (
                candidates.T, counts.T,
                tokens.reshape(tiles, TILE, TILE), centroids.reshape(local, TILE, TILE),
                row_mass.reshape(2, half, TILE), col_mass.reshape(local, TILE),
            )
        )
    )
    return qd.reshape(-1), cd.reshape(-1), out.reshape(tokens.shape)


def solution(mesh):
    in_specs = (
        P("row", None),
        P("col", None),
        P("row"),
        P("col"),
        P("row", "col"),
        P("row", "col"),
    )
    out_specs = (P("row"), P("col"), P("row", None))
    body = functools.partial(shards, mesh.shape["row"], mesh.shape["col"] // 2)
    return jax.shard_map(body, mesh=mesh, in_specs=in_specs, out_specs=out_specs, check_vma=False)
```

```python
import functools
import math

import jax
import jax.numpy as jnp
from jax import lax
from jax.experimental import pallas as pl
from jax.experimental.pallas import tpu as pltpu
from jax.sharding import PartitionSpec as P

TILE = 128
SLOTS = 4
ITERS = 2
CHUNKS = 8
EPS = 0.025
OFFSET = 0.5
MESH = pl.DeviceIdType.MESH
F32 = jnp.float32
BF16 = jnp.bfloat16
NT = (((1,), (1,)), ((), ()))
TN = (((0,), (0,)), ((), ()))


def unit(values):
    wide = values.astype(F32)
    factor = lax.rsqrt(jnp.mean(wide * wide, axis=-1, keepdims=True) + 1e-06)
    return (wide * factor).astype(BF16)


def spread(row, rows=16):
    return jnp.broadcast_to(row, (rows, TILE)).astype(BF16)


def column(row):
    return jnp.transpose(jnp.broadcast_to(row, (TILE, TILE)))


def remote(src, dst, ss, rs, where):
    copy = pltpu.make_async_remote_copy(
        src_ref=src, dst_ref=dst, send_sem=ss, recv_sem=rs, device_id=where, device_id_type=MESH
    )
    copy.start()
    return copy


def wait_bytes(ref, sem):
    pltpu.make_async_copy(ref, ref, sem).wait()


def kernel(
    nrow, nz, tiles, local, qt,
    cand, cnt, tok, cen, rmass, cmass,
    qd, cd, out,
    tokv, cenv, rmv, cmv, cu, kb, cc, hot, psum, pair, zrow, rsc, qsum, crow, csc,
    pd, dpair, dsum, drow, nb, npair, fr, br,
    in_s, row_s, col_s, d_s, d_r, np_s, np_r, ring_s, ring_r, ag_s, ag_r, sh_s, sh_r,
):
    half = tiles // 2
    hq = qt // 2
    r = lax.axis_index("row")
    k = lax.axis_index("col")
    z = k // 2
    c = k % 2
    o = 1 - c
    partner = {"col": 2 * z + o}
    up = {"col": 2 * lax.rem(z + 1, nz) + c}
    down = {"col": 2 * lax.rem(z + nz - 1, nz) + c}
    up2 = {"col": 2 * lax.rem(z + 2, nz) + c}
    down2 = {"col": 2 * lax.rem(z + nz - 2, nz) + c}

    barrier = pltpu.get_barrier_semaphore()
    pl.semaphore_signal(barrier, inc=1, device_id=partner, device_id_type=MESH)
    for d in range(1, nz):
        pl.semaphore_signal(
            barrier, inc=1, device_id={"col": 2 * lax.rem(z + d, nz) + c}, device_id_type=MESH
        )
    for d in range(1, nrow):
        pl.semaphore_signal(barrier, inc=1, device_id={"row": lax.rem(r + d, nrow)}, device_id_type=MESH)

    chunk = tiles // CHUNKS
    load = pltpu.make_async_copy(cen, cenv, in_s.at[CHUNKS])
    load.start()
    for h in (o, c):
        for n in range(CHUNKS // 2):
            at = pl.ds(h * half + n * chunk, chunk)
            pltpu.make_async_copy(tok.at[at], tokv.at[at], in_s.at[h * (CHUNKS // 2) + n]).start()
    masses = [
        pltpu.make_async_copy(rmass, rmv, in_s.at[CHUNKS + 1]),
        pltpu.make_async_copy(cmass, cmv, in_s.at[CHUNKS + 2]),
    ]
    for copy in masses:
        copy.start()

    load.wait()

    @pl.loop(0, local, unroll=4)
    def _(n):
        cu[n] = unit(cenv[n])

    lane = lax.broadcasted_iota(jnp.int32, (1, TILE), 1)
    scale = math.log2(math.e) / (TILE * EPS)
    shift = -OFFSET / EPS * math.log2(math.e)

    def fill(h):
        @pl.loop(0, CHUNKS // 2)
        def _(n):
            first = h * half + n * chunk
            at = pl.ds(first, chunk)
            pltpu.make_async_copy(tok.at[at], tokv.at[at], in_s.at[h * (CHUNKS // 2) + n]).wait()

            @pl.loop(0, chunk, unroll=8)
            def _(m):
                one_tile(h, n * chunk + m, first + m)

    def one_tile(h, g, t):
        tu = unit(tokv[t])
        listed = cnt[0, t]
        chosen = [cand[s, t] for s in range(SLOTS)]
        picked = jnp.concatenate([cu[x] for x in chosen], axis=0)
        sims = lax.dot_general(tu, picked, NT, preferred_element_type=F32)
        total = None
        for s in range(SLOTS):
            base = jnp.minimum(listed - (s + 1), 0).astype(F32) * 1e30 + shift
            gibbs = jnp.exp2(sims[:, s * TILE : (s + 1) * TILE] * scale + base)
            kb[t, :, s * TILE : (s + 1) * TILE] = gibbs.astype(BF16)
            total = gibbs if total is None else total + gibbs
            hot[s, pl.ds(t, 1), :] = (lane == chosen[s]).astype(F32)
        sums = jnp.transpose(jnp.sum(total, axis=1, keepdims=True))
        psum[0, h, pl.ds(g, 1), :] = sums

    def row_send(i):
        return remote(psum.at[i, o], pair.at[i], row_s.at[i, 0], row_s.at[i, 1], partner)

    def row_exchange(i, sent):
        sent.wait()
        zrow[i, z] = (psum[i, c] + pair[i]).astype(BF16)
        for d in sorted(range(1, nz), key=lambda d: -min(d, nz - d)):
            there = {"col": 2 * lax.rem(z + d, nz) + c}
            remote(zrow.at[i, z], zrow.at[i, z], row_s.at[i, 2], row_s.at[i, 3], there)
        wait_bytes(zrow.at[i, pl.ds(0, nz - 1)], row_s.at[i, 3])
        whole = zrow[i, 0].astype(F32)
        for d in range(1, nz):
            whole = whole + zrow[i, d].astype(F32)
        rsc[i, c] = rmv[c] / whole
        shared = remote(rsc.at[i, c], rsc.at[i, c], row_s.at[i, 4], row_s.at[i, 5], partner)
        wait_bytes(zrow.at[i, pl.ds(0, nz - 1)], row_s.at[i, 2])
        return shared

    fill(o)
    pl.semaphore_wait(barrier, nz + nrow - 1)
    sent = row_send(0)
    fill(c)
    for copy in masses:
        copy.wait()

    def col_exchange(i):
        side = math.isqrt(nrow)
        hops = lambda d: min(d // side, side - d // side) + min(d % side, side - d % side)
        for d in sorted(range(1, nrow), key=lambda d: -hops(d)):
            remote(crow.at[i, r], crow.at[i, r], col_s.at[i, 0], col_s.at[i, 1], {"row": lax.rem(r + d, nrow)})
        wait_bytes(crow.at[i, pl.ds(0, nrow - 1)], col_s.at[i, 1])
        wait_bytes(crow.at[i, pl.ds(0, nrow - 1)], col_s.at[i, 0])
        whole = crow[i, 0].astype(F32)
        for d in range(1, nrow):
            whole = whole + crow[i, d].astype(F32)
        csc[i] = cmv[...] / whole

    for i in range(ITERS):
        if i > 0:
            scales = jnp.concatenate([csc[i - 1], jnp.zeros((TILE - local, TILE), F32)], axis=0).astype(BF16)
            for s in range(SLOTS):
                qsum[s] = jnp.dot(hot[s].astype(BF16), scales, preferred_element_type=F32)

            def row_pass(h):
                @pl.loop(0, half, unroll=8)
                def _(g):
                    t = h * half + g
                    weight = jnp.concatenate([spread(qsum[s, pl.ds(t, 1), :]) for s in range(SLOTS)], axis=1)
                    sums = lax.dot_general(weight, kb[t], NT, preferred_element_type=F32)
                    psum[i, h, pl.ds(g, 1), :] = sums[0:1, :]

            row_pass(o)
            sent = row_send(i)
            row_pass(c)

        shared = row_exchange(i, sent)

        def col_pass(h):
            @pl.loop(0, half, unroll=8)
            def _(g):
                t = h * half + g
                weight = spread(rsc[i, h, pl.ds(g, 1), :])
                sums = jnp.dot(weight, kb[t], preferred_element_type=F32)
                for s in range(SLOTS):
                    qsum[s, pl.ds(t, 1), :] = sums[0:1, s * TILE : (s + 1) * TILE]

        col_pass(c)
        shared.wait()
        col_pass(o)
        whole = jnp.zeros((TILE, TILE), F32)
        for s in range(SLOTS):
            pick = hot[s].astype(BF16)
            high = qsum[s].astype(BF16)
            low = (qsum[s] - high.astype(F32)).astype(BF16)
            whole = whole + lax.dot_general(pick, high, TN, preferred_element_type=F32)
            whole = whole + lax.dot_general(pick, low, TN, preferred_element_type=F32)
        crow[i, r] = whole[0:local, :].astype(BF16)
        col_exchange(i)

    last = ITERS - 1

    @pl.loop(0, local, unroll=4)
    def _(n):
        wide = column(csc[last, pl.ds(n, 1), :] * (1.0 / 16.0))
        cc[n, :, 0:TILE] = (wide * cu[n].astype(F32)).astype(BF16)
        cc[n, :, TILE : 2 * TILE] = wide.astype(BF16)

    diagonal = lax.broadcasted_iota(jnp.int32, (TILE, TILE), 0) == lax.broadcasted_iota(
        jnp.int32, (TILE, TILE), 1
    )

    def numerators(h, g):
        for q in range(qt):
            t = h * half + g * qt + q
            scaled = jnp.concatenate([cc[cand[s, t]] for s in range(SLOTS)], axis=0)
            acc = jnp.dot(kb[t], scaled, preferred_element_type=F32)
            nb[h, g, q] = acc[:, 0:TILE].astype(BF16)
            mass = jnp.where(diagonal, acc[:, TILE : 2 * TILE], 0.0)
            pd[h, g, q : q + 1, :] = jnp.sum(mass, axis=0, keepdims=True)

    def group(d):
        return lax.rem(z + d, nz)

    sends = []
    far = nz // 2
    order = [far] + [x for j in range(1, far) for x in (far - j, far + j)] + [0]

    def give(d):
        j, g = order.index(d), group(d)
        numerators(o, g)
        sends.append(remote(nb.at[o, g], npair.at[g], np_s.at[j], np_r.at[j], partner))
        sends.append(remote(pd.at[o, g], dpair.at[g], d_s.at[0, j], d_r.at[j], partner))

    def take(d):
        j, g = order.index(d), group(d)
        wait_bytes(npair.at[g], np_r.at[j])
        wait_bytes(dpair.at[g], d_r.at[j])
        dsum[g] = pd[c, g] + dpair[g]
        if d == 0:
            drow[z] = dsum[z]
        else:
            sends.append(remote(dsum.at[g], drow.at[z], d_s.at[1, j], d_r.at[nz], {"col": 2 * g + c}))

    def ring(side, step, q):
        buf = (fr, br)[side]
        to = ((up2, down2) if step == 0 else (up, down))[side]
        g = group(far - step if side == 0 else far + step)
        value = nb[c, g, q].astype(F32) + npair[g, q].astype(F32)
        came = [step - 1] if step > 1 else []
        if step == 2 and (q < hq) == (side == 0):
            came.append(0)
        for n in came:
            wait_bytes(buf.at[n, q], ring_r.at[side, n, q])
            value = value + buf[n, q].astype(F32)
        nb[c, g, q] = value.astype(BF16)
        sends.append(
            remote(nb.at[c, g, q], buf.at[step, q], ring_s.at[side, step, q], ring_r.at[side, step, q], to)
        )

    first, second = list(range(hq)), list(range(hq, qt))
    give(far)
    give(far - 1)
    give(far + 1)
    numerators(c, group(far))
    take(far)
    for a, b in zip(first, second):
        ring(0, 0, a)
        ring(1, 0, b)
    for step in range(1, far):
        if step > 1:
            give(far - step)
            give(far + step)
        numerators(c, group(far - step))
        numerators(c, group(far + step))
        if step == far - 1:
            give(0)
        take(far - step)
        take(far + step)
        for a, b in zip(second + first, first + second):
            ring(0, step, a)
            ring(1, step, b)
    numerators(c, z)
    take(0)

    wait_bytes(drow.at[pl.ds(0, nz - 1)], d_r.at[nz])
    mass = drow[0]
    for d in range(1, nz):
        mass = mass + drow[d]

    final = far - 1
    for q in range(qt):
        value = nb[c, z, q].astype(F32) + npair[z, q].astype(F32)
        scale_out = 1.0 / column(mass[q : q + 1, :])
        wait_bytes(fr.at[final, q], ring_r.at[0, final, q])
        wait_bytes(br.at[final, q], ring_r.at[1, final, q])
        value = value + fr[final, q].astype(F32) + br[final, q].astype(F32)
        out[c, z, q] = (value * scale_out).astype(BF16)
        ref = out.at[c, z, q]
        sends.append(remote(ref, ref, ag_s.at[0, 0, q], ag_r.at[0, 0, q], up))
        sends.append(remote(ref, ref, ag_s.at[1, 0, q], ag_r.at[1, 0, q], down))

    def share(n, ref):
        sends.append(remote(ref, ref, sh_s.at[n], sh_r, partner))

    share(0, out.at[c, z])
    for dist in range(1, far + 1):
        for q in range(qt):
            for side, g, to, to2 in ((0, group(nz - dist), up, up2), (1, group(dist), down, down2)):
                longest = (q < hq) == (side == 0)
                if dist == far and not longest:
                    continue
                ref = out.at[c, g, q]
                wait_bytes(ref, ag_r.at[side, dist - 1, q])
                if dist == far - 2 and longest:
                    sends.append(remote(ref, ref, ag_s.at[side, far - 1, q], ag_r.at[side, far - 1, q], to2))
                if dist < far - 1:
                    sends.append(remote(ref, ref, ag_s.at[side, dist, q], ag_r.at[side, dist, q], to))
        if dist < far:
            share(2 * dist - 1, out.at[c, group(nz - dist)])
            share(2 * dist, out.at[c, group(dist)])
        else:
            share(2 * far - 1, out.at[c, group(far)])

    qd[...] = EPS * jnp.log(rsc[last])
    cd[...] = EPS * jnp.log(csc[last])

    wait_bytes(out.at[o], sh_r)
    for copy in sends:
        copy.wait_send()


def shards(nrow, nz, tokens, centroids, row_mass, col_mass, candidates, counts):
    tiles = tokens.shape[0] // TILE
    local = centroids.shape[0] // TILE
    half = tiles // 2
    qt = half // nz
    far = nz // 2
    vmem = pl.BlockSpec(memory_space=pltpu.VMEM)
    hbm = pl.BlockSpec(memory_space=pltpu.HBM)
    smem = pl.BlockSpec(memory_space=pltpu.SMEM)
    dma = pltpu.SemaphoreType.DMA
    qd, cd, out = pl.pallas_call(
        functools.partial(kernel, nrow, nz, tiles, local, qt),
        out_shape=(
            jax.ShapeDtypeStruct((2, half, TILE), F32),
            jax.ShapeDtypeStruct((local, TILE), F32),
            jax.ShapeDtypeStruct((2, nz, qt, TILE, TILE), BF16),
        ),
        in_specs=[smem, smem, hbm, hbm, hbm, hbm],
        out_specs=(vmem, vmem, vmem),
        scratch_shapes=[
            pltpu.VMEM((tiles, TILE, TILE), BF16),
            pltpu.VMEM((local, TILE, TILE), BF16),
            pltpu.VMEM((2, half, TILE), F32),
            pltpu.VMEM((local, TILE), F32),
            pltpu.VMEM((local, TILE, TILE), BF16),
            pltpu.VMEM((tiles, TILE, SLOTS * TILE), BF16),
            pltpu.VMEM((local, TILE, 2 * TILE), BF16),
            pltpu.VMEM((SLOTS, tiles, TILE), F32),
            pltpu.VMEM((ITERS, 2, half, TILE), F32),
            pltpu.VMEM((ITERS, half, TILE), F32),
            pltpu.VMEM((ITERS, nz, half, TILE), BF16),
            pltpu.VMEM((ITERS, 2, half, TILE), F32),
            pltpu.VMEM((SLOTS, tiles, TILE), F32),
            pltpu.VMEM((ITERS, nrow, local, TILE), BF16),
            pltpu.VMEM((ITERS, local, TILE), F32),
            pltpu.VMEM((2, nz, qt, TILE), F32),
            pltpu.VMEM((nz, qt, TILE), F32),
            pltpu.VMEM((nz, qt, TILE), F32),
            pltpu.VMEM((nz, qt, TILE), F32),
            pltpu.VMEM((2, nz, qt, TILE, TILE), BF16),
            pltpu.VMEM((nz, qt, TILE, TILE), BF16),
            pltpu.VMEM((far, qt, TILE, TILE), BF16),
            pltpu.VMEM((far, qt, TILE, TILE), BF16),
            dma((CHUNKS + 3,)),
            dma((ITERS, 6)),
            dma((ITERS, 2)),
            dma((2, nz)),
            dma((nz + 1,)),
            dma((nz,)),
            dma((nz,)),
            dma((2, far, qt)),
            dma((2, far, qt)),
            dma((2, far, qt)),
            dma((2, far, qt)),
            dma((nz,)),
            dma(()),
        ],
        compiler_params=pltpu.CompilerParams(
            collective_id=0, has_side_effects=True, vmem_limit_bytes=36 << 20
        ),
    )(
        *(
            pltpu.with_memory_space_constraint(x, pltpu.HBM)
            for x in (
                candidates.T, counts.T,
                tokens.reshape(tiles, TILE, TILE), centroids.reshape(local, TILE, TILE),
                row_mass.reshape(2, half, TILE), col_mass.reshape(local, TILE),
            )
        )
    )
    return qd.reshape(-1), cd.reshape(-1), out.reshape(tokens.shape)


def solution(mesh):
    in_specs = (
        P("row", None),
        P("col", None),
        P("row"),
        P("col"),
        P("row", "col"),
        P("row", "col"),
    )
    out_specs = (P("row"), P("col"), P("row", None))
    body = functools.partial(shards, mesh.shape["row"], mesh.shape["col"] // 2)
    return jax.shard_map(body, mesh=mesh, in_specs=in_specs, out_specs=out_specs, check_vma=False)
```
